32 devices in a mesh: wide: 8 (over z, x), narrow: 4 (over y, core).
Axes of the slice: x: 2, y: 2, z: 4, core: 2. Of those that a mesh axis runs over, the one named last changes fastest.
Arguments:
- node: bfloat16 [256, 256, 256], P('narrow'), may hold values from -6 to 6
- right_side: bfloat16 [256, 256, 256], P('narrow'), may hold values from -16 to 16
- leg_ops: bfloat16 [3, 12, 256, 256], replicated, may hold values from -0.375 to 0.375
- op_index: int32 [32, 3], P('wide'), may hold values from 0 to 11, as said below
- offsets: int32 [32], P('wide'), may hold values from 0 to 7
Outputs:
- new_node: float32 [256, 256, 256], P('narrow')
The draws below stay inside these ranges and needn't reach their ends.
Inputs may be any that keep to these rules, and one draw needn't show every extreme that they name: `op_index`: no two triples name the same pair of leg b and leg c operators; every operator of each leg is named by some triple.
All inputs are finite; a program needn't handle non-finite values.
Results may differ from the reference program's by a relative error of at most 0.0019.
Values may be sent and summed in bfloat16 or wider, within the bound.
A program may use at most 192 MiB of HBM per device.

```python
import math
import jax
import jax.numpy as jnp

BOND = 256
KOPS = 12
SECTORS = 8
TRIPLES = 32


def draw_op_index(key, part):
    subkeys = jax.random.split(jax.random.fold_in(key, 7321), 5)
    position = jnp.arange(TRIPLES, dtype=jnp.int32)
    perm_a = jax.random.permutation(subkeys[0], KOPS).astype(jnp.int32)
    perm_b = jax.random.permutation(subkeys[1], KOPS).astype(jnp.int32)
    perm_c = jax.random.permutation(subkeys[2], KOPS).astype(jnp.int32)
    slot_row = position % KOPS
    slot_col = (position // KOPS + position % KOPS) % KOPS
    filler = jax.random.randint(subkeys[3], (TRIPLES,), 0, KOPS).astype(jnp.int32)
    leg_a = jnp.where(position < KOPS, perm_a[slot_row], filler)
    lookup_table = jnp.stack([leg_a, perm_b[slot_row], perm_c[slot_col]], axis=1)
    shuffle = jax.random.permutation(subkeys[4], TRIPLES).astype(jnp.int32)
    return lookup_table[shuffle].astype(jnp.int32)


def place_ends(entries, own_key, smallest, top_value):
    shape = entries.shape
    index_at = [jax.random.randint(jax.random.fold_in(own_key, axis), (), 0, shape[axis]) for axis in range(len(shape))]
    entries = entries.at[tuple(index_at)].set(smallest)
    longest = shape.index(max(shape))
    index_at[longest] = (index_at[longest] + 1) % shape[longest]
    return entries.at[tuple(index_at)].set(top_value)


def level_of(rng, dims, shards, low, high):
    loudness, own = 1.0, jax.random.fold_in(rng, 6)
    for dim, parts in shards:
        heights = jnp.exp(jax.random.uniform(jax.random.fold_in(own, dim), (parts,), jnp.float32, low / len(shards), high / len(shards)))
        loudness = loudness * jnp.repeat(heights, dims[dim] // parts).reshape([-1 if axis == dim else 1 for axis in range(len(dims))])
    return loudness


def centred(rng, extent, width, most, cuts=(), held_as=jnp.bfloat16):
    result = jax.random.normal(rng, extent, jnp.float32) * width
    if len(cuts) > 0:
        result = level_of(rng, extent, cuts, -0.22, 0.18) * result
    return jnp.clip(result, min=-most, max=most).astype(held_as)


def setup_inputs(seed: int = 0) -> dict:
    arg_keys = jax.random.split(jax.random.key(seed), 6)
    return {
        "node": centred(arg_keys[0], (BOND, BOND, BOND), 1.0, 6.0, ((0, 4),)),
        "right_side": centred(arg_keys[1], (BOND, BOND, BOND), 4.0, 16.0, ((0, 4),)),
        "leg_ops": centred(arg_keys[2], (3, KOPS, BOND, BOND), BOND ** -0.5, 0.375),
        "op_index": draw_op_index(jax.random.fold_in(arg_keys[5], 71), 0),
        "offsets": place_ends(jax.random.randint(arg_keys[4], (TRIPLES,), 0, SECTORS), jax.random.fold_in(arg_keys[4], 1), 0, SECTORS - 1).astype(jnp.int32),
    }


def reference(node, right_side, leg_ops, op_index, offsets):
    whole = node.astype(jnp.float32)
    sector = BOND // SECTORS
    sigma = jnp.zeros((BOND, BOND, BOND), jnp.float32)
    for triple in range(TRIPLES):
        op_a = leg_ops[0, op_index[triple, 0]].astype(jnp.float32)
        op_b = leg_ops[1, op_index[triple, 1]].astype(jnp.float32)
        op_c = leg_ops[2, op_index[triple, 2]].astype(jnp.float32)
        first = jnp.einsum('abc,qc->abq', whole, op_c).astype(jnp.bfloat16).astype(jnp.float32)
        second = jnp.einsum('pb,abq->apq', op_b, first).astype(jnp.bfloat16).astype(jnp.float32)
        shifted = jnp.roll(op_a, offsets[triple] * sector, axis=0)
        sigma = sigma + jnp.einsum('ra,apq->rpq', shifted, second)
    tau = 0.5 / math.sqrt(TRIPLES)
    return whole + tau * (right_side.astype(jnp.float32) - sigma)
```

```python
import functools
import math

import jax
import jax.numpy as jnp
from jax import lax
from jax.experimental import pallas as pl
from jax.experimental.pallas import tpu as pltpu
from jax.sharding import PartitionSpec as P

SECTORS = 8
NT = (((1,), (1,)), ((), ()))


def sum_kernel(triples, parts, sector, table, first, ops_b, ops_a, out, op_a, second):
    block, rows, bond = first.shape[1:]
    group = max(1, 128 // rows)

    @pl.when(pl.program_id(0) == 0)
    def _():
        def shift(step, carry):
            pieces = []
            for place in range(group):
                triple = step * group + place
                start = pl.multiple_of(bond - table[triple, 3] * sector, sector)
                pieces.append(ops_a[table[triple, 0], pl.ds(start, bond), :])
            lanes = group * rows
            at = pl.multiple_of(step * lanes, lanes)
            op_a[:, pl.ds(at, lanes)] = jnp.concatenate(pieces, axis=1)
            return carry

        lax.fori_loop(0, triples // group, shift, 0)

    def leg_b(triple, carry):
        value = first[table[triple, 2]].reshape(block * rows, bond)
        result = lax.dot_general(
            value, ops_b[table[triple, 1]], NT, preferred_element_type=jnp.float32
        )
        at = pl.multiple_of(triple * rows, rows)
        second[:, pl.ds(at, rows), :] = result.astype(jnp.bfloat16).reshape(block, rows, bond)
        return carry

    lax.fori_loop(0, triples, leg_b, 0, unroll=4)

    def leg_a(place, carry):
        result = jnp.dot(op_a[...], second[place], preferred_element_type=jnp.float32)
        result = result.astype(jnp.bfloat16).reshape(parts, rows, bond)
        out[:, place] = result
        return carry

    lax.fori_loop(0, block, leg_a, 0)


def partial_sums(first, ops_b, ops_a, table, parts, sector):
    kops, width, rows, bond = first.shape
    triples = table.shape[0]
    block = min(width, max(1, 256 // rows))
    return pl.pallas_call(
        functools.partial(sum_kernel, triples, parts, sector),
        out_shape=jax.ShapeDtypeStruct((parts, width, rows, bond), jnp.bfloat16),
        grid_spec=pltpu.PrefetchScalarGridSpec(
            num_scalar_prefetch=1,
            grid=(width // block,),
            in_specs=[
                pl.BlockSpec((kops, block, rows, bond), lambda i, t: (0, i, 0, 0)),
                pl.BlockSpec(ops_b.shape, lambda i, t: (0, 0, 0)),
                pl.BlockSpec(ops_a.shape, lambda i, t: (0, 0, 0)),
            ],
            out_specs=pl.BlockSpec((parts, block, rows, bond), lambda i, t: (0, i, 0, 0)),
            scratch_shapes=[
                pltpu.VMEM((bond, triples * rows), jnp.bfloat16),
                pltpu.VMEM((block, triples * rows, bond), jnp.bfloat16),
            ],
        ),
        compiler_params=pltpu.CompilerParams(vmem_limit_bytes=40 * 2**20),
    )(table, first, ops_b, ops_a)


def per_device(node, right_side, leg_ops, op_index, offsets):
    rows, bond = node.shape[0], node.shape[1]
    sector = bond // SECTORS
    wide, narrow = lax.axis_size("wide"), lax.axis_size("narrow")
    triples = op_index.shape[0] * wide
    tau = 0.5 / math.sqrt(triples)
    width = bond // wide
    table = jnp.concatenate([op_index, offsets[:, None]], axis=1)
    table = lax.all_gather(table, "wide", axis=0, tiled=True)
    ops_c = lax.dynamic_slice_in_dim(leg_ops[2], lax.axis_index("wide") * width, width, 1)
    ops_a = lax.dynamic_slice_in_dim(leg_ops[0], lax.axis_index("narrow") * rows, rows, 2)
    ops_a = jnp.concatenate([ops_a, ops_a], axis=1)
    first = jnp.einsum("kqc,abc->kqab", ops_c, node, preferred_element_type=jnp.float32).astype(
        jnp.bfloat16
    )
    partial_value = partial_sums(first, leg_ops[1], ops_a, table, narrow, sector)
    share = lax.psum_scatter(partial_value, "narrow", scatter_dimension=0, tiled=False)
    sigma = lax.all_gather(share, "wide", axis=0, tiled=True)
    sigma = jnp.transpose(sigma, (1, 2, 0)).astype(jnp.float32)
    return node.astype(jnp.float32) + tau * (right_side.astype(jnp.float32) - sigma)


def solution(mesh):
    in_specs = (P("narrow", None, None), P("narrow", None, None), P(), P("wide", None), P("wide"))
    out_specs = P("narrow", None, None)
    return jax.shard_map(
        per_device, mesh=mesh, in_specs=in_specs, out_specs=out_specs, check_vma=False
    )
```

```python
import functools
import math

import jax
import jax.numpy as jnp
from jax import lax
from jax.experimental import pallas as pl
from jax.experimental.pallas import tpu as pltpu
from jax.sharding import PartitionSpec as P

SECTORS = 8
NT = (((1,), (1,)), ((), ()))


def sum_kernel(triples, parts, sector, table, first, ops_b, ops_a, out, op_a, second):
    block, rows, bond = first.shape[1:]
    group = max(1, 128 // rows)

    @pl.when(pl.program_id(0) == 0)
    def _():
        def shift(step, carry):
            pieces = []
            for place in range(group):
                triple = step * group + place
                start = pl.multiple_of(bond - table[triple, 3] * sector, sector)
                pieces.append(ops_a[table[triple, 0], pl.ds(start, bond), :])
            lanes = group * rows
            at = pl.multiple_of(step * lanes, lanes)
            op_a[:, pl.ds(at, lanes)] = jnp.concatenate(pieces, axis=1)
            return carry

        lax.fori_loop(0, triples // group, shift, 0)

    def leg_b(triple, carry):
        value = first[table[triple, 2]].reshape(block * rows, bond)
        result = lax.dot_general(
            value, ops_b[table[triple, 1]], NT, preferred_element_type=jnp.float32
        )
        at = pl.multiple_of(triple * rows, rows)
        second[:, pl.ds(at, rows), :] = result.astype(jnp.bfloat16).reshape(block, rows, bond)
        return carry

    lax.fori_loop(0, triples, leg_b, 0, unroll=4)

    def leg_a(place, carry):
        result = jnp.dot(op_a[...], second[place], preferred_element_type=jnp.float32)
        result = result.astype(jnp.bfloat16).reshape(parts, rows, bond)
        out[:, place] = result
        return carry

    lax.fori_loop(0, block, leg_a, 0)


def partial_sums(first, ops_b, ops_a, table, parts, sector):
    kops, width, rows, bond = first.shape
    triples = table.shape[0]
    block = min(width, max(1, 256 // rows))
    return pl.pallas_call(
        functools.partial(sum_kernel, triples, parts, sector),
        out_shape=jax.ShapeDtypeStruct((parts, width, rows, bond), jnp.bfloat16),
        grid_spec=pltpu.PrefetchScalarGridSpec(
            num_scalar_prefetch=1,
            grid=(width // block,),
            in_specs=[
                pl.BlockSpec((kops, block, rows, bond), lambda i, t: (0, i, 0, 0)),
                pl.BlockSpec(ops_b.shape, lambda i, t: (0, 0, 0)),
                pl.BlockSpec(ops_a.shape, lambda i, t: (0, 0, 0)),
            ],
            out_specs=pl.BlockSpec((parts, block, rows, bond), lambda i, t: (0, i, 0, 0)),
            scratch_shapes=[
                pltpu.VMEM((bond, triples * rows), jnp.bfloat16),
                pltpu.VMEM((block, triples * rows, bond), jnp.bfloat16),
            ],
        ),
        compiler_params=pltpu.CompilerParams(vmem_limit_bytes=40 * 2**20),
    )(table, first, ops_b, ops_a)


def update_kernel(tau, node, right_side, sigma, out):
    bond = node.shape[1]
    for row in range(node.shape[0]):
        value = sigma[:, row].reshape(bond, bond).astype(jnp.float32).T
        right = right_side[row].astype(jnp.float32)
        out[row] = node[row].astype(jnp.float32) + tau * (right - value)


def update(node, right_side, sigma, tau):
    rows, bond = node.shape[:2]
    wide, _, width, _ = sigma.shape
    block = min(rows, 8)
    whole = pl.BlockSpec((block, bond, bond), lambda i: (i, 0, 0))
    return pl.pallas_call(
        functools.partial(update_kernel, tau),
        out_shape=jax.ShapeDtypeStruct(node.shape, jnp.float32),
        grid=(rows // block,),
        in_specs=[
            whole,
            whole,
            pl.BlockSpec((wide, block, width, bond), lambda i: (0, i, 0, 0)),
        ],
        out_specs=whole,
        compiler_params=pltpu.CompilerParams(vmem_limit_bytes=40 * 2**20),
    )(node, right_side, sigma)


def per_device(node, right_side, leg_ops, op_index, offsets):
    rows, bond = node.shape[0], node.shape[1]
    sector = bond // SECTORS
    wide, narrow = lax.axis_size("wide"), lax.axis_size("narrow")
    triples = op_index.shape[0] * wide
    tau = 0.5 / math.sqrt(triples)
    width = bond // wide
    table = jnp.concatenate([op_index, offsets[:, None]], axis=1)
    pieces = [table]
    for step in range(1, wide):
        ring = [(place, (place + step) % wide) for place in range(wide)]
        pieces.append(lax.ppermute(table, "wide", ring))
    table = jnp.concatenate(pieces, axis=0)
    ops_c = lax.dynamic_slice_in_dim(leg_ops[2], lax.axis_index("wide") * width, width, 1)
    ops_a = lax.dynamic_slice_in_dim(leg_ops[0], lax.axis_index("narrow") * rows, rows, 2)
    ops_a = jnp.concatenate([ops_a, ops_a], axis=1)
    first = jnp.einsum("kqc,abc->kqab", ops_c, node, preferred_element_type=jnp.float32).astype(
        jnp.bfloat16
    )
    partial_value = partial_sums(first, leg_ops[1], ops_a, table, narrow, sector)
    share = lax.psum_scatter(partial_value, "narrow", scatter_dimension=0, tiled=False)
    share = jnp.swapaxes(share, 0, 1)
    sigma = lax.all_gather(share, "wide", axis=0, tiled=True).reshape((wide,) + share.shape)
    return update(node, right_side, sigma, tau)


def solution(mesh):
    in_specs = (P("narrow", None, None), P("narrow", None, None), P(), P("wide", None), P("wide"))
    out_specs = P("narrow", None, None)
    return jax.shard_map(
        per_device, mesh=mesh, in_specs=in_specs, out_specs=out_specs, check_vma=False
    )
```

```python
import functools
import math

import jax
import jax.numpy as jnp
from jax import lax
from jax.experimental import pallas as pl
from jax.experimental.pallas import tpu as pltpu
from jax.sharding import PartitionSpec as P

SECTORS = 8
NT = (((1,), (1,)), ((), ()))


def sum_kernel(triples, parts, sector, table, first, ops_b, ops_a, out, op_a, second):
    block, rows, bond = first.shape[1:]
    group = max(1, 128 // rows)

    @pl.when(pl.program_id(0) == 0)
    def _():
        def shift(step, carry):
            pieces = []
            for place in range(group):
                triple = step * group + place
                start = pl.multiple_of(bond - table[triple, 3] * sector, sector)
                pieces.append(ops_a[table[triple, 0], pl.ds(start, bond), :])
            lanes = group * rows
            at = pl.multiple_of(step * lanes, lanes)
            op_a[:, pl.ds(at, lanes)] = jnp.concatenate(pieces, axis=1)
            return carry

        lax.fori_loop(0, triples // group, shift, 0)

    def leg_b(triple, carry):
        value = first[table[triple, 2]].reshape(block * rows, bond)
        result = lax.dot_general(
            value, ops_b[table[triple, 1]], NT, preferred_element_type=jnp.float32
        )
        at = pl.multiple_of(triple * rows, rows)
        second[:, pl.ds(at, rows), :] = result.astype(jnp.bfloat16).reshape(block, rows, bond)
        return carry

    lax.fori_loop(0, triples, leg_b, 0, unroll=4)

    def leg_a(place, carry):
        result = jnp.dot(op_a[...], second[place], preferred_element_type=jnp.float32)
        result = result.astype(jnp.bfloat16).reshape(parts, rows, bond)
        out[:, place] = result
        return carry

    lax.fori_loop(0, block, leg_a, 0)


def partial_sums(first, ops_b, ops_a, table, parts, sector):
    kops, width, rows, bond = first.shape
    triples = table.shape[0]
    block = min(width, max(1, 256 // rows))
    return pl.pallas_call(
        functools.partial(sum_kernel, triples, parts, sector),
        out_shape=jax.ShapeDtypeStruct((parts, width, rows, bond), jnp.bfloat16),
        grid_spec=pltpu.PrefetchScalarGridSpec(
            num_scalar_prefetch=1,
            grid=(width // block,),
            in_specs=[
                pl.BlockSpec((kops, block, rows, bond), lambda i, t: (0, i, 0, 0)),
                pl.BlockSpec(ops_b.shape, lambda i, t: (0, 0, 0)),
                pl.BlockSpec(ops_a.shape, lambda i, t: (0, 0, 0)),
            ],
            out_specs=pl.BlockSpec((parts, block, rows, bond), lambda i, t: (0, i, 0, 0)),
            scratch_shapes=[
                pltpu.VMEM((bond, triples * rows), jnp.bfloat16),
                pltpu.VMEM((block, triples * rows, bond), jnp.bfloat16),
            ],
        ),
        compiler_params=pltpu.CompilerParams(vmem_limit_bytes=40 * 2**20),
    )(table, first, ops_b, ops_a)


def swap_kernel(value, out):
    out[...] = jnp.swapaxes(value[...].astype(jnp.float32), 0, 1).astype(out.dtype)


def swap_leading(value):
    width, rows, bond = value.shape
    return pl.pallas_call(
        swap_kernel,
        out_shape=jax.ShapeDtypeStruct((rows, width, bond), value.dtype),
        compiler_params=pltpu.CompilerParams(vmem_limit_bytes=24 * 2**20),
    )(value)


def update_kernel(tau, node, right_side, sigma, out):
    bond = node.shape[1]
    for row in range(node.shape[0]):
        value = sigma[:, row].reshape(bond, bond).astype(jnp.float32).T
        right = right_side[row].astype(jnp.float32)
        out[row] = node[row].astype(jnp.float32) + tau * (right - value)


def update(node, right_side, sigma, tau):
    rows, bond = node.shape[:2]
    wide, _, width, _ = sigma.shape
    block = min(rows, 8)
    whole = pl.BlockSpec((block, bond, bond), lambda i: (i, 0, 0))
    return pl.pallas_call(
        functools.partial(update_kernel, tau),
        out_shape=jax.ShapeDtypeStruct(node.shape, jnp.float32),
        grid=(rows // block,),
        in_specs=[
            whole,
            whole,
            pl.BlockSpec((wide, block, width, bond), lambda i: (0, i, 0, 0)),
        ],
        out_specs=whole,
        compiler_params=pltpu.CompilerParams(vmem_limit_bytes=40 * 2**20),
    )(node, right_side, sigma)


def per_device(node, right_side, leg_ops, op_index, offsets):
    rows, bond = node.shape[0], node.shape[1]
    sector = bond // SECTORS
    wide, narrow = lax.axis_size("wide"), lax.axis_size("narrow")
    triples = op_index.shape[0] * wide
    tau = 0.5 / math.sqrt(triples)
    width = bond // wide
    table = jnp.concatenate([op_index, offsets[:, None]], axis=1)
    pieces = [table]
    for step in range(1, wide):
        ring = [(place, (place + step) % wide) for place in range(wide)]
        pieces.append(lax.ppermute(table, "wide", ring))
    table = jnp.concatenate(pieces, axis=0)
    ops_c = lax.dynamic_slice_in_dim(leg_ops[2], lax.axis_index("wide") * width, width, 1)
    ops_a = lax.dynamic_slice_in_dim(leg_ops[0], lax.axis_index("narrow") * rows, rows, 2)
    ops_a = jnp.concatenate([ops_a, ops_a], axis=1)
    first = jnp.einsum("kqc,abc->kqab", ops_c, node, preferred_element_type=jnp.float32).astype(
        jnp.bfloat16
    )
    partial_value = partial_sums(first, leg_ops[1], ops_a, table, narrow, sector)
    share = lax.psum_scatter(partial_value, "narrow", scatter_dimension=0, tiled=False)
    share = swap_leading(share)
    sigma = lax.all_gather(share, "wide", axis=0, tiled=True).reshape((wide,) + share.shape)
    return update(node, right_side, sigma, tau)


def solution(mesh):
    in_specs = (P("narrow", None, None), P("narrow", None, None), P(), P("wide", None), P("wide"))
    out_specs = P("narrow", None, None)
    return jax.shard_map(
        per_device, mesh=mesh, in_specs=in_specs, out_specs=out_specs, check_vma=False
    )
```
